128 devices in a mesh: phase: 4 (over z_hi, core), dp: 32 (over x, y, z_lo).
Axes of the slice: x: 4, y: 4, z: 4 (z_hi: 2, z_lo: 2; z = z_hi * 2 + z_lo), core: 2. Of those that a mesh axis runs over, the one named last changes fastest.
Arguments:
- query_key_value_blocks: bfloat16 [4, 32, 2, 128, 10240], P('phase', 'dp'), may hold values from -18 to 18
- row_document_index: int32 [4, 32, 2, 128], P('phase', 'dp'), may hold values from 0 to 3, never falling along the last dimension, each value on 1 to 64 neighbouring positions
- counts: int32 [4, 32], P('phase', 'dp'), may hold values from 1 to 2
- block_adapter_index: int32 [4, 32, 2], P('phase'), may hold values from 0 to 31
- lowrank_down_weight: bfloat16 [4, 32, 8192, 64], P('phase', None, 'dp'), may hold values from -0.0625 to 0.0625
- lowrank_up_weight: bfloat16 [4, 32, 64, 8192], P('phase', None, None, 'dp'), may hold values from -0.75 to 0.75
- cotangent: bfloat16 [4, 32, 2, 128, 8192], P('phase', None, None, None, 'dp'), may hold values from -0.1796875 to 0.1796875
Outputs:
- delta: bfloat16 [4, 32, 2, 128, 8192], P('phase', None, None, None, 'dp')
- grad_down: float32 [4, 32, 8192, 64], P('phase', None, 'dp')
- grad_up: float32 [4, 32, 64, 8192], P('phase', None, None, 'dp')
The draws below stay inside these ranges and needn't reach their ends.
Inputs may be any that keep to these rules, and one draw needn't show every extreme that they name: `row_document_index`: each row lies in one document; documents of a block are consecutive rows, at most 64 rows each.
All inputs are finite; a program needn't handle non-finite values.
Results may differ from the reference program's by a relative error of at most 0.0061.
Values may be sent and summed in bfloat16 or wider, within the bound.
A program may use at most 128 MiB of HBM per device.

```python
import math
import jax
import jax.numpy as jnp
import numpy as np
from jax import lax

MODEL_WIDTH = 8192
HEADS = 64
KV_HEADS = 8
HEAD_DIM = 128
ADAPTER_RANK = 64
BLOCK = 128
SLOTS = 2
ADAPTER_TOTAL = 32
RELAY_SECTIONS = 4
BINS = 32


def draw_query_key_value_blocks(key, part):
    key = jax.random.fold_in(key, 11)
    columns = (HEADS + 2 * KV_HEADS) * HEAD_DIM
    block_shape = (RELAY_SECTIONS, BINS, SLOTS, BLOCK, columns)
    full = jnp.clip(jax.random.normal(key, block_shape, jnp.float32), -6.0, 6.0)
    return full.astype(jnp.bfloat16)


def set_ends(entries, rng, smallest, largest):
    extent = entries.shape
    spot = [jax.random.randint(jax.random.fold_in(rng, axis), (), 0, extent[axis]) for axis in range(len(extent))]
    entries = entries.at[tuple(spot)].set(smallest)
    longest = extent.index(max(extent))
    spot[longest] = (spot[longest] + 1) % extent[longest]
    return entries.at[tuple(spot)].set(largest)


def level_of(own_key, dims, shards, least, top_value):
    factor_of = 1.0
    for axis_at, shards_of in shards:
        steps = jax.random.uniform(jax.random.fold_in(jax.random.fold_in(own_key, 6), axis_at), (shards_of,), jnp.float32, least / len(shards), top_value / len(shards))
        factor_of = factor_of * jnp.repeat(jnp.exp(steps), dims[axis_at] // shards_of).reshape((-1,) + (1,) * (len(dims) - 1 - axis_at))
    return factor_of


def cumulative_ranks(number_of, slope):
    loads = [(1 << 20) // math.isqrt(standing ** slope) + 1 for standing in range(1, number_of + 1)]
    deviation = 1 + sum(loads) // (1 << 30)
    return np.cumsum(np.array([max(1, weight // deviation) for weight in loads]))


def skewed_ids(stream_key, extent, number_of, slope):
    table = cumulative_ranks(number_of, slope)
    pick = jax.random.randint(jax.random.fold_in(stream_key, 1), extent, 0, int(table[number_of - 1]))
    rank = jnp.searchsorted(jnp.asarray(table, jnp.int32), pick, side="right")
    return jax.random.permutation(jax.random.fold_in(stream_key, 2), number_of)[rank].astype(jnp.int32)


def split_up(count, total, most, lean):
    portions = [(1 << 20) // math.isqrt(rank ** lean) + 1 for rank in range(2, count + 1)]
    rest, given = total - most - (count - 1), [1] * (count - 1)
    while rest > 0:
        candidates = [i for i in range(count - 1) if given[i] < most]
        whole, budget = sum([portions[i] for i in candidates]), rest
        for i in candidates:
            more = min(most - given[i], max(1, budget * portions[i] // whole), rest)
            given[i] = given[i] + more
            rest = rest - more
    return np.array([most] + given)


def uneven(key, number_of, total, limit, slope):
    if number_of == 2:
        one = jax.random.randint(key, (), max(1, total - limit), min(limit, total - 1) + 1)
        return jnp.stack([one, total - one])
    tallies = jnp.asarray(split_up(number_of, total, limit, slope), jnp.int32)
    twos = (number_of - 1) // 2
    source_of, receiver = tallies[1:1 + 2 * twos:2], tallies[2:2 + 2 * twos:2]
    margin = jnp.minimum(source_of - 1, limit - receiver)
    shifted = jax.random.randint(jax.random.fold_in(key, 1), (twos,), 0, 1 << 20) % (margin + 1)
    tallies = tallies.at[1:1 + 2 * twos:2].set(source_of - shifted).at[2:2 + 2 * twos:2].set(receiver + shifted)
    return tallies[jax.random.permutation(jax.random.fold_in(key, 2), number_of)]


def noise(key, dims, spread, most, shards=(), held_as=jnp.bfloat16):
    level = level_of(key, dims, shards, -0.22, 0.18) if shards else 1.0
    entries = jax.random.normal(key, dims, jnp.float32) * spread * level
    return jnp.minimum(jnp.maximum(entries, -most), most).astype(held_as)


def setup_inputs(seed: int = 0) -> dict:
    arg_keys = jax.random.split(jax.random.key(seed), 8)
    query_key_value_blocks = draw_query_key_value_blocks(jax.random.fold_in(arg_keys[7], 71), 0)
    row_document_index = jax.vmap(lambda own: jnp.searchsorted(jnp.cumsum(uneven(own, 4, BLOCK, BLOCK // 2, 2)), jnp.arange(BLOCK), side="right"))(jax.random.split(arg_keys[1], RELAY_SECTIONS * BINS * SLOTS)).reshape((RELAY_SECTIONS, BINS, SLOTS, BLOCK)).astype(jnp.int32)
    counts = set_ends(jax.random.randint(arg_keys[2], (RELAY_SECTIONS, BINS), 1, SLOTS + 1), jax.random.fold_in(arg_keys[2], 1), 1, SLOTS).astype(jnp.int32)
    block_adapter_index = set_ends(skewed_ids(arg_keys[3], (RELAY_SECTIONS, BINS, SLOTS), ADAPTER_TOTAL, 2), jax.random.fold_in(arg_keys[3], 3), 0, ADAPTER_TOTAL - 1).astype(jnp.int32)
    lowrank_down_weight = noise(arg_keys[4], (RELAY_SECTIONS, ADAPTER_TOTAL, MODEL_WIDTH, ADAPTER_RANK), MODEL_WIDTH ** -0.5, 0.0625, ((0, 4), (2, 32)))
    lowrank_up_weight = noise(arg_keys[5], (RELAY_SECTIONS, ADAPTER_TOTAL, ADAPTER_RANK, MODEL_WIDTH), ADAPTER_RANK ** -0.5, 0.75, ((0, 4), (3, 32)))
    cotangent = noise(arg_keys[6], (RELAY_SECTIONS, BINS, SLOTS, BLOCK, MODEL_WIDTH), 0.03, 0.1796875, ((0, 4), (4, 32)))
    return {"query_key_value_blocks": query_key_value_blocks, "row_document_index": row_document_index, "counts": counts, "block_adapter_index": block_adapter_index, "lowrank_down_weight": lowrank_down_weight, "lowrank_up_weight": lowrank_up_weight, "cotangent": cotangent}


LOWRANK_SCALE = 2.0


def attend(qkv_rows, documents, alive_mask):
    group_size = HEADS // KV_HEADS
    queries = qkv_rows[:, :, :HEADS * HEAD_DIM].astype(jnp.float32).reshape(SLOTS, BLOCK, KV_HEADS, group_size, HEAD_DIM)
    key_rows = qkv_rows[:, :, HEADS * HEAD_DIM:(HEADS + KV_HEADS) * HEAD_DIM].astype(jnp.float32).reshape(SLOTS, BLOCK, KV_HEADS, HEAD_DIM)
    value_rows = qkv_rows[:, :, (HEADS + KV_HEADS) * HEAD_DIM:].astype(jnp.float32).reshape(SLOTS, BLOCK, KV_HEADS, HEAD_DIM)
    scores = jnp.einsum('sikgd,sjkd->skgij', queries, key_rows) * (HEAD_DIM ** -0.5)
    position = jnp.arange(BLOCK)
    allowed = (documents[:, :, None] == documents[:, None, :]) & (position[None, None, :] <= position[None, :, None])
    scores = jnp.where(allowed[:, None, None, :, :], scores, -1e30)
    row_max = jnp.max(scores, axis=-1, keepdims=True)
    powers = jnp.exp(scores - row_max)
    weights = (powers / jnp.sum(powers, axis=-1, keepdims=True)).astype(jnp.bfloat16)
    weights = lax.optimization_barrier(weights).astype(jnp.float32)
    mixed = jnp.einsum('skgij,sjkd->sikgd', weights, value_rows).reshape(SLOTS, BLOCK, HEADS * HEAD_DIM)
    return (mixed * alive_mask[:, None, None]).astype(jnp.bfloat16)


def attend_items(items):
    return attend(items[0], items[1], items[2])


def reference(query_key_value_blocks, row_document_index, counts, block_adapter_index, lowrank_down_weight, lowrank_up_weight, cotangent):
    arriving = jnp.roll(query_key_value_blocks, 1, axis=0)
    slot_index = jnp.arange(SLOTS)
    highest = lax.Precision.HIGHEST
    delta_list = []
    down_list = []
    up_list = []
    for relay_section in range(RELAY_SECTIONS):
        alive_mask = (slot_index[None, :] < counts[relay_section][:, None]).astype(jnp.float32)
        mixed = lax.map(attend_items, (arriving[relay_section], row_document_index[relay_section], alive_mask))
        mixed_wide = mixed.astype(jnp.float32)
        adapter_indicator = (block_adapter_index[relay_section][:, :, None] == jnp.arange(ADAPTER_TOTAL)[None, None, :]).astype(jnp.float32)
        selected_down_weight = jnp.take(lowrank_down_weight[relay_section], block_adapter_index[relay_section], axis=0).astype(jnp.float32)
        selected_up_weight = jnp.take(lowrank_up_weight[relay_section], block_adapter_index[relay_section], axis=0).astype(jnp.float32)
        projected_rows = jnp.einsum('psiw,pswr->psir', mixed_wide, selected_down_weight)
        scaled_rows = (LOWRANK_SCALE * projected_rows).astype(jnp.bfloat16)
        scaled_wide = lax.optimization_barrier(scaled_rows).astype(jnp.float32)
        delta = jnp.einsum('psir,psrw->psiw', scaled_wide, selected_up_weight).astype(jnp.bfloat16)
        grad_rows = cotangent[relay_section].astype(jnp.float32)
        backward_rows = jnp.einsum('psiw,psrw->psir', grad_rows, selected_up_weight)
        backward_scaled_rows = (LOWRANK_SCALE * backward_rows).astype(jnp.bfloat16)
        back_wide = lax.optimization_barrier(backward_scaled_rows).astype(jnp.float32)
        per_up = jnp.einsum('psir,psiw->psrw', scaled_wide, grad_rows)
        grad_up = jnp.einsum('psa,psrw->arw', adapter_indicator, per_up, precision=highest)
        per_down = jnp.einsum('psiw,psir->pswr', mixed_wide, back_wide)
        grad_down = jnp.einsum('psa,pswr->awr', adapter_indicator, per_down, precision=highest)
        delta_list.append(delta)
        down_list.append(grad_down)
        up_list.append(grad_up)
    return (jnp.stack(delta_list), jnp.stack(down_list), jnp.stack(up_list))
```

```python
import math

import jax
import jax.numpy as jnp
from jax import lax
from jax.experimental import pallas as pl
from jax.experimental.pallas import tpu as pltpu
from jax.sharding import PartitionSpec as P

HEADS = 64
KV_HEADS = 8
HEAD_DIM = 128
GROUP = HEADS // KV_HEADS
WIDTH = HEADS * HEAD_DIM
RANK = 64
ROWS = 128
SLOTS = 2
SECTIONS = 4
BINS = 32
BLOCKS = BINS * SLOTS
SHARD = WIDTH // BINS
ADAPTERS = 32
LOWRANK_SCALE = 2.0
C_CHUNKS = 4
G_EARLY = 16
MESH = pl.DeviceIdType.MESH
F32 = jnp.float32
BF16 = jnp.bfloat16


def dot(a, b, ca, cb):
    return lax.dot_general(
        a, b, (((ca,), (cb,)), ((), ())), preferred_element_type=F32
    )


def partner(me, step):
    kz, kx = step // 16, step % 4
    ky = ((step // 4) % 4 + 4 - kx) % 4
    x, y, z = me // 8, (me // 2) % 4, me % 2
    return ((x + kx) % 4) * 8 + ((y + ky) % 4) * 2 + (z + kz) % 2


def owner_kernel(
    index_ref, info_ref, up_ref, down_ref, cot_hbm, qkv_hbm,
    scaled_out, grad_out,
    cot, qkv, info_in, bias, back_send, back_recv, down_send, down_recv, mixed, scaled, grad_send,
    cot_sem, qkv_sem, info_sem, back_sem, down_sem, scaled_sem, grad_sem,
):
    phase, me = lax.axis_index("phase"), lax.axis_index("dp")
    owners, shards = (phase + SECTIONS - 1) % SECTIONS, (phase + 1) % SECTIONS

    def remote(src, dst, sem, section, to):
        return pltpu.make_async_remote_copy(
            src_ref=src, dst_ref=dst, send_sem=sem.at[0], recv_sem=sem.at[1],
            device_id=(section, to), device_id_type=MESH,
        )

    per_chunk = BLOCKS // C_CHUNKS

    def cot_copy(chunk):
        at = pl.ds(chunk * per_chunk, per_chunk)
        return pltpu.make_async_copy(cot_hbm.at[at], cot.at[at], cot_sem.at[chunk])

    for chunk in range(C_CHUNKS):
        cot_copy(chunk).start()
    qkv_copy = pltpu.make_async_copy(qkv_hbm, qkv, qkv_sem)
    qkv_copy.start()

    barrier = pltpu.get_barrier_semaphore()

    def greet(step, _):
        pl.semaphore_signal(
            barrier, inc=1, device_id=(shards, partner(me, step)), device_id_type=MESH
        )
        return 0

    lax.fori_loop(0, BINS, greet, 0)

    for chunk in range(C_CHUNKS):
        cot_copy(chunk).wait()

        def back_part(owner, _):
            for slot in range(SLOTS):
                up = up_ref[index_ref[slot, owner]]
                part = dot(up, cot[owner * SLOTS + slot], 1, 1)
                back_send[owner, :, slot * ROWS : (slot + 1) * ROWS] = part.astype(BF16)
            return 0

        lax.fori_loop(
            chunk * per_chunk // SLOTS, (chunk + 1) * per_chunk // SLOTS, back_part, 0
        )

    pl.semaphore_wait(barrier, BINS)
    info_copy = remote(info_ref, info_in, info_sem, owners, me)
    info_copy.start()

    def send_back(step, _):
        to = partner(me, step)
        remote(back_send.at[to], back_recv.at[me], back_sem, owners, to).start()
        return 0

    lax.fori_loop(0, BINS, send_back, 0)

    def send_down(step, _):
        to = partner(me, step)
        for slot in range(SLOTS):
            down_send[to, slot * RANK : (slot + 1) * RANK] = down_ref[index_ref[slot, to]]
        remote(down_send.at[to], down_recv.at[me], down_sem, owners, to).start()
        return 0

    lax.fori_loop(0, BINS, send_down, 0)

    info_copy.wait()
    row = lax.broadcasted_iota(jnp.int32, (ROWS, ROWS), 0)
    column = lax.broadcasted_iota(jnp.int32, (ROWS, ROWS), 1)
    for slot in range(SLOTS):
        documents = jnp.broadcast_to(info_in[slot : slot + 1, :].astype(F32), (ROWS, ROWS))
        kept = (documents == documents.T) & (column <= row)
        bias[slot] = jnp.where(kept, 0.0, -1e30)
    qkv_copy.wait()
    to_power_of_two = math.log2(math.e) * HEAD_DIM**-0.5

    def attend(step, _):
        slot, kv = step // KV_HEADS, step % KV_HEADS
        alive = jnp.where(info_in[SLOTS : SLOTS + 1, :] > slot, 1.0, 0.0)
        keys = qkv[slot, :, pl.ds(pl.multiple_of(WIDTH + kv * HEAD_DIM, HEAD_DIM), HEAD_DIM)]
        values = qkv[
            slot, :, pl.ds(pl.multiple_of(WIDTH + (KV_HEADS + kv) * HEAD_DIM, HEAD_DIM), HEAD_DIM)
        ]
        values_and_ones = jnp.concatenate([values, jnp.ones_like(values)], axis=1)
        for head in range(GROUP):
            at = pl.ds(pl.multiple_of((kv * GROUP + head) * HEAD_DIM, HEAD_DIM), HEAD_DIM)
            scores = dot(qkv[slot, :, at], keys, 1, 1) + bias[slot]
            top = jnp.max(scores, axis=-1, keepdims=True)
            powers = jnp.exp2((scores - top) * to_power_of_two).astype(BF16)
            both = dot(powers, values_and_ones, 1, 0)
            mixed[slot, :, at] = (
                both[:, :HEAD_DIM] * (alive / both[:, HEAD_DIM:])
            ).astype(BF16)
        return 0

    lax.fori_loop(0, SLOTS * KV_HEADS, attend, 0)

    remote(back_send, back_recv, back_sem, owners, me).wait_recv()

    def add_back(source, total):
        return total + back_recv[source].astype(F32)

    back = lax.fori_loop(0, BINS, add_back, jnp.zeros((RANK, SLOTS * ROWS), F32))
    back_scaled = (LOWRANK_SCALE * back).astype(BF16)

    def send_grad(step, _):
        to = partner(me, step)
        at = pl.ds(pl.multiple_of(to * SHARD, SHARD), SHARD)
        for slot in range(SLOTS):
            part = dot(back_scaled[:, slot * ROWS : (slot + 1) * ROWS], mixed[slot, :, at], 1, 0)
            grad_send[to, slot * RANK : (slot + 1) * RANK] = part.astype(BF16)
        remote(grad_send.at[to], grad_out.at[me], grad_sem, shards, to).start()
        return 0

    def project(source, totals):
        at = pl.ds(pl.multiple_of(source * SHARD, SHARD), SHARD)
        return tuple(
            totals[slot]
            + dot(down_recv[source, slot * RANK : (slot + 1) * RANK], mixed[slot, :, at], 1, 1)
            for slot in range(SLOTS)
        )

    lax.fori_loop(0, G_EARLY, send_grad, 0)
    remote(down_send, down_recv, down_sem, owners, me).wait_recv()
    projected = lax.fori_loop(
        0, BINS, project, tuple(jnp.zeros((RANK, ROWS), F32) for _ in range(SLOTS))
    )
    for slot in range(SLOTS):
        scaled[:, slot * ROWS : (slot + 1) * ROWS] = (LOWRANK_SCALE * projected[slot]).astype(BF16)

    def send_scaled(step, _):
        to = partner(me, step)
        remote(scaled, scaled_out.at[me], scaled_sem, shards, to).start()
        return 0

    lax.fori_loop(0, BINS, send_scaled, 0)
    lax.fori_loop(G_EARLY, BINS, send_grad, 0)

    remote(back_send, back_recv, back_sem, owners, me).wait_send()
    remote(down_send, down_recv, down_sem, owners, me).wait_send()
    whole_grad = remote(grad_send, grad_out, grad_sem, shards, me)
    whole_scaled = remote(back_send, scaled_out, scaled_sem, shards, me)
    whole_scaled.wait_recv()
    whole_scaled.wait_send()
    whole_grad.wait_recv()
    whole_grad.wait_send()


def owner_call(index, info, up, down, cotangent, qkv):
    vmem, hbm = pl.BlockSpec(memory_space=pltpu.VMEM), pl.BlockSpec(memory_space=pl.ANY)
    return pl.pallas_call(
        owner_kernel,
        out_shape=(
            jax.ShapeDtypeStruct((BINS, RANK, SLOTS * ROWS), BF16),
            jax.ShapeDtypeStruct((BINS, SLOTS * RANK, SHARD), BF16),
        ),
        in_specs=[pl.BlockSpec(memory_space=pltpu.SMEM), vmem, vmem, vmem, hbm, hbm],
        out_specs=(hbm, hbm),
        scratch_shapes=[
            pltpu.VMEM((BLOCKS, ROWS, SHARD), BF16),
            pltpu.VMEM(qkv.shape, BF16),
            pltpu.VMEM((8, ROWS), jnp.int32),
            pltpu.VMEM((SLOTS, ROWS, ROWS), F32),
            pltpu.VMEM((BINS, RANK, SLOTS * ROWS), BF16),
            pltpu.VMEM((BINS, RANK, SLOTS * ROWS), BF16),
            pltpu.VMEM((BINS, SLOTS * RANK, SHARD), BF16),
            pltpu.VMEM((BINS, SLOTS * RANK, SHARD), BF16),
            pltpu.VMEM((SLOTS, ROWS, WIDTH), BF16),
            pltpu.VMEM((RANK, SLOTS * ROWS), BF16),
            pltpu.VMEM((BINS, SLOTS * RANK, SHARD), BF16),
            pltpu.SemaphoreType.DMA((C_CHUNKS,)),
            pltpu.SemaphoreType.DMA,
            pltpu.SemaphoreType.DMA((2,)),
            pltpu.SemaphoreType.DMA((2,)),
            pltpu.SemaphoreType.DMA((2,)),
            pltpu.SemaphoreType.DMA((2,)),
            pltpu.SemaphoreType.DMA((2,)),
        ],
        compiler_params=pltpu.CompilerParams(
            collective_id=0, has_side_effects=True, vmem_limit_bytes=48 << 20
        ),
        name="owner",
    )(index, info, up, down, cotangent, qkv)


STEP_BLOCKS = 8


def shard_kernel(index_ref, scaled_ref, grad_ref, cot_ref, up_ref, delta_ref, down_out, up_out):
    step = pl.program_id(0)

    @pl.when(step == 0)
    def _():
        down_out[...] = jnp.zeros_like(down_out)
        up_out[...] = jnp.zeros_like(up_out)

    for at in range(STEP_BLOCKS):
        bin_at, slot = at // SLOTS, at % SLOTS
        adapter = index_ref[slot, step * (STEP_BLOCKS // SLOTS) + bin_at]
        scaled = scaled_ref[bin_at, :, slot * ROWS : (slot + 1) * ROWS]
        delta_ref[at] = dot(scaled, up_ref[adapter], 0, 0).astype(BF16)
        up_out[adapter] += dot(scaled, cot_ref[at], 1, 0)
        down_out[adapter] += grad_ref[bin_at, slot * RANK : (slot + 1) * RANK].astype(F32)


def shard_call(index, scaled, grad, cotangent, up):
    bins = STEP_BLOCKS // SLOTS
    whole = pl.BlockSpec((ADAPTERS, RANK, SHARD), lambda i, _: (0, 0, 0))
    return pl.pallas_call(
        shard_kernel,
        out_shape=(
            jax.ShapeDtypeStruct((BLOCKS, ROWS, SHARD), BF16),
            jax.ShapeDtypeStruct((ADAPTERS, RANK, SHARD), F32),
            jax.ShapeDtypeStruct((ADAPTERS, RANK, SHARD), F32),
        ),
        grid_spec=pltpu.PrefetchScalarGridSpec(
            num_scalar_prefetch=1,
            grid=(BLOCKS // STEP_BLOCKS,),
            in_specs=[
                pl.BlockSpec((bins, RANK, SLOTS * ROWS), lambda i, _: (i, 0, 0)),
                pl.BlockSpec((bins, SLOTS * RANK, SHARD), lambda i, _: (i, 0, 0)),
                pl.BlockSpec((STEP_BLOCKS, ROWS, SHARD), lambda i, _: (i, 0, 0)),
                whole,
            ],
            out_specs=(
                pl.BlockSpec((STEP_BLOCKS, ROWS, SHARD), lambda i, _: (i, 0, 0)),
                whole,
                whole,
            ),
        ),
        compiler_params=pltpu.CompilerParams(vmem_limit_bytes=40 << 20),
        name="shard",
    )(index, scaled, grad, cotangent, up)


def on_device(
    query_key_value_blocks,
    row_document_index,
    counts,
    block_adapter_index,
    lowrank_down_weight,
    lowrank_up_weight,
    cotangent,
):
    index = block_adapter_index[0].T
    info = jnp.concatenate(
        [
            row_document_index[0, 0],
            jnp.broadcast_to(counts, (8 - SLOTS, ROWS)),
        ]
    )
    up = lowrank_up_weight[0]
    down = lowrank_down_weight[0].transpose(0, 2, 1)
    cot = cotangent.reshape(BLOCKS, ROWS, SHARD)
    scaled, grad = owner_call(index, info, up, down, cot, query_key_value_blocks[0, 0])
    delta, grad_down, grad_up = shard_call(index, scaled, grad, cot, up)
    return (
        delta.reshape(cotangent.shape),
        grad_down.transpose(0, 2, 1)[None],
        grad_up[None],
    )


def solution(mesh):
    in_specs = (
        P("phase", "dp", None, None, None),
        P("phase", "dp", None, None),
        P("phase", "dp"),
        P("phase", None, None),
        P("phase", None, "dp", None),
        P("phase", None, None, "dp"),
        P("phase", None, None, None, "dp"),
    )
    out_specs = (
        P("phase", None, None, None, "dp"),
        P("phase", None, "dp", None),
        P("phase", None, None, "dp"),
    )
    return jax.shard_map(
        on_device, mesh=mesh, in_specs=in_specs, out_specs=out_specs, check_vma=False
    )
```

```python
import math

import jax
import jax.numpy as jnp
from jax import lax
from jax.experimental import pallas as pl
from jax.experimental.pallas import tpu as pltpu
from jax.sharding import PartitionSpec as P

HEADS = 64
KV_HEADS = 8
HEAD_DIM = 128
GROUP = HEADS // KV_HEADS
WIDTH = HEADS * HEAD_DIM
RANK = 64
ROWS = 128
SLOTS = 2
SECTIONS = 4
BINS = 32
BLOCKS = BINS * SLOTS
SHARD = WIDTH // BINS
ADAPTERS = 32
LOWRANK_SCALE = 2.0
MESH = pl.DeviceIdType.MESH
F32 = jnp.float32
BF16 = jnp.bfloat16


def hold(array):
    return pltpu.with_memory_space_constraint(array, pltpu.HBM)


def dot(a, b, ca, cb):
    return lax.dot_general(
        a, b, (((ca,), (cb,)), ((), ())), preferred_element_type=F32
    )


def partner(me, step):
    kx, turn = step % 4, (step // 4) % 4
    ky, kz = (turn + 4 - kx) % 4, (step // 16 + turn + kx) % 2
    x, y, z = me // 8, (me // 2) % 4, me % 2
    return ((x + kx) % 4) * 8 + ((y + ky) % 4) * 2 + (z + kz) % 2


def owner_kernel(
    index_hbm, documents_hbm, counts_hbm, up_hbm, down_hbm, cot_hbm, qkv_hbm,
    grad_out, delta_out, per_up_out,
    index_ref, counts_ref, up_ref, down_ref, cot, qkv, documents_own, info_own, info_in, bias,
    back_send, back_recv, down_send, down_recv, mixed, scaled, scaled_in, grad_send,
    load_sem, info_sem, back_sem, down_sem, scaled_sem, grad_sem,
):
    phase, me = lax.axis_index("phase"), lax.axis_index("dp")
    owners, shards = (phase + SECTIONS - 1) % SECTIONS, (phase + 1) % SECTIONS

    def remote(src, dst, sem, section, to):
        return pltpu.make_async_remote_copy(
            src_ref=src, dst_ref=dst, send_sem=sem.at[0], recv_sem=sem.at[1],
            device_id=(section, to), device_id_type=MESH,
        )

    loads = [
        pltpu.make_async_copy(src, dst, load_sem.at[i])
        for i, (src, dst) in enumerate(
            (
                (index_hbm, index_ref),
                (counts_hbm, counts_ref),
                (documents_hbm, documents_own),
                (down_hbm, down_ref),
                (up_hbm, up_ref),
                (cot_hbm, cot),
                (qkv_hbm, qkv),
            )
        )
    ]
    for load in loads:
        load.start()
    index_load, counts_load, documents_load, down_load, up_load, cot_load, qkv_load = loads

    barrier = pltpu.get_barrier_semaphore()

    def greet(step, _):
        pl.semaphore_signal(
            barrier, inc=1, device_id=(shards, partner(me, step)), device_id_type=MESH
        )
        return 0

    lax.fori_loop(0, BINS, greet, 0)

    counts_load.wait()
    documents_load.wait()
    info_own[...] = jnp.full(info_own.shape, counts_ref[0, 0], jnp.int32)
    info_own[:SLOTS] = documents_own[...]
    index_load.wait()
    down_load.wait()

    def choose_down(to, _):
        for slot in range(SLOTS):
            down_send[to, slot * RANK : (slot + 1) * RANK] = down_ref[index_ref[slot, to]]
        return 0

    lax.fori_loop(0, BINS, choose_down, 0, unroll=4)

    pl.semaphore_wait(barrier, BINS)
    info_copy = remote(info_own, info_in, info_sem, owners, me)
    info_copy.start()

    def send_down(step, _):
        to = partner(me, step)
        remote(down_send.at[to], down_recv.at[me], down_sem, owners, to).start()
        return 0


    up_load.wait()
    cot_load.wait()

    def send_back(step, _):
        to = partner(me, step)
        for slot in range(SLOTS):
            part = dot(up_ref[index_ref[slot, to]], cot[to * SLOTS + slot], 1, 1)
            back_send[to, :, slot * ROWS : (slot + 1) * ROWS] = part.astype(BF16)
        remote(back_send.at[to], back_recv.at[me], back_sem, owners, to).start()
        return 0

    lax.fori_loop(0, BINS, send_back, 0, unroll=4)

    lax.fori_loop(0, BINS, send_down, 0)

    info_copy.wait()
    row = lax.broadcasted_iota(jnp.int32, (ROWS, ROWS), 0)
    column = lax.broadcasted_iota(jnp.int32, (ROWS, ROWS), 1)
    for slot in range(SLOTS):
        documents = jnp.broadcast_to(info_in[slot : slot + 1, :].astype(F32), (ROWS, ROWS))
        kept = (documents == documents.T) & (column <= row)
        bias[slot] = jnp.where(kept, 0.0, -1e30)
    qkv_load.wait()
    to_power_of_two = math.log2(math.e) * HEAD_DIM**-0.5

    def attend(step, _):
        slot, kv = step // KV_HEADS, step % KV_HEADS
        alive = jnp.where(info_in[SLOTS : SLOTS + 1, :] > slot, 1.0, 0.0)
        keys = qkv[slot, :, pl.ds(pl.multiple_of(WIDTH + kv * HEAD_DIM, HEAD_DIM), HEAD_DIM)]
        values = qkv[
            slot, :, pl.ds(pl.multiple_of(WIDTH + (KV_HEADS + kv) * HEAD_DIM, HEAD_DIM), HEAD_DIM)
        ]
        heads = [
            pl.ds(pl.multiple_of((kv * GROUP + head) * HEAD_DIM, HEAD_DIM), HEAD_DIM)
            for head in range(GROUP)
        ]
        queries = jnp.concatenate([qkv[slot, :, at] for at in heads], axis=0)
        scores = dot(queries, keys, 1, 1).reshape(GROUP, ROWS, ROWS) + bias[slot]
        top = jnp.max(scores, axis=-1, keepdims=True)
        powers = jnp.exp2((scores - top) * to_power_of_two)
        weights = powers * (1.0 / jnp.sum(powers, axis=-1, keepdims=True))
        weights = weights.astype(BF16).reshape(GROUP * ROWS, ROWS)
        group = (dot(weights, values, 1, 0) * alive).astype(BF16)
        for head, at in enumerate(heads):
            mixed[slot, :, at] = group[head * ROWS : (head + 1) * ROWS]
        return 0

    lax.fori_loop(0, SLOTS * KV_HEADS, attend, 0, unroll=2)

    def piece(which):
        at = pl.ds(pl.multiple_of(which * SHARD, SHARD), SHARD)
        return mixed[:, :, at].reshape(SLOTS * ROWS, SHARD)

    def project(source, total):
        return total + dot(down_recv[source], piece(source), 1, 1)

    remote(down_send, down_recv, down_sem, owners, me).wait_recv()
    projected = lax.fori_loop(
        0, BINS, project, jnp.zeros((SLOTS * RANK, SLOTS * ROWS), F32), unroll=4
    )
    for slot in range(SLOTS):
        at = slice(slot * ROWS, (slot + 1) * ROWS)
        own = projected[slot * RANK : (slot + 1) * RANK, at]
        scaled[:, at] = (LOWRANK_SCALE * own).astype(BF16)

    def send_scaled(step, _):
        to = partner(me, step)
        remote(scaled, scaled_in.at[me], scaled_sem, shards, to).start()
        return 0

    lax.fori_loop(0, BINS, send_scaled, 0)

    remote(back_send, back_recv, back_sem, owners, me).wait_recv()

    def add_back(source, total):
        return total + back_recv[source].astype(F32)

    back = lax.fori_loop(0, BINS, add_back, jnp.zeros((RANK, SLOTS * ROWS), F32), unroll=4)
    back_scaled = (LOWRANK_SCALE * back).astype(BF16)
    nothing = jnp.zeros((RANK, ROWS), BF16)
    back_diagonal = jnp.concatenate(
        [
            jnp.concatenate([back_scaled[:, :ROWS], nothing], axis=1),
            jnp.concatenate([nothing, back_scaled[:, ROWS:]], axis=1),
        ],
        axis=0,
    )

    def send_grad(step, _):
        to = partner(me, step)
        grad_send[to] = dot(back_diagonal, piece(to), 1, 0).astype(BF16)
        remote(grad_send.at[to], grad_out.at[me], grad_sem, shards, to).start()
        return 0

    lax.fori_loop(0, BINS, send_grad, 0, unroll=4)

    whole_scaled = remote(back_send, scaled_in, scaled_sem, shards, me)
    whole_scaled.wait_recv()

    def spread(source, _):
        for slot in range(SLOTS):
            block = source * SLOTS + slot
            own = scaled_in[source, :, slot * ROWS : (slot + 1) * ROWS]
            delta_out[block] = dot(own, up_ref[index_ref[slot, source]], 0, 0).astype(BF16)
            per_up_out[block] = dot(own, cot[block], 1, 0)
        return 0

    lax.fori_loop(0, BINS, spread, 0, unroll=2)

    remote(back_send, back_recv, back_sem, owners, me).wait_send()
    remote(down_send, down_recv, down_sem, owners, me).wait_send()
    whole_scaled.wait_send()
    whole_grad = remote(grad_send, grad_out, grad_sem, shards, me)
    whole_grad.wait_recv()
    whole_grad.wait_send()


def owner_call(index, documents, counts, up, down, cotangent, qkv):
    vmem, hbm = pl.BlockSpec(memory_space=pltpu.VMEM), pl.BlockSpec(memory_space=pl.ANY)
    return pl.pallas_call(
        owner_kernel,
        out_shape=(
            jax.ShapeDtypeStruct((BINS, SLOTS * RANK, SHARD), BF16),
            jax.ShapeDtypeStruct((BLOCKS, ROWS, SHARD), BF16),
            jax.ShapeDtypeStruct((BLOCKS, RANK, SHARD), F32),
        ),
        in_specs=[pl.BlockSpec(memory_space=pltpu.HBM)] * 7,
        out_specs=(hbm, vmem, vmem),
        scratch_shapes=[
            pltpu.SMEM((SLOTS, BINS), jnp.int32),
            pltpu.SMEM((1, 1), jnp.int32),
            pltpu.VMEM((ADAPTERS, RANK, SHARD), BF16),
            pltpu.VMEM((ADAPTERS, RANK, SHARD), BF16),
            pltpu.VMEM((BLOCKS, ROWS, SHARD), BF16),
            pltpu.VMEM(qkv.shape, BF16),
            pltpu.VMEM((SLOTS, ROWS), jnp.int32),
            pltpu.VMEM((8, ROWS), jnp.int32),
            pltpu.VMEM((8, ROWS), jnp.int32),
            pltpu.VMEM((SLOTS, ROWS, ROWS), F32),
            pltpu.VMEM((BINS, RANK, SLOTS * ROWS), BF16),
            pltpu.VMEM((BINS, RANK, SLOTS * ROWS), BF16),
            pltpu.VMEM((BINS, SLOTS * RANK, SHARD), BF16),
            pltpu.VMEM((BINS, SLOTS * RANK, SHARD), BF16),
            pltpu.VMEM((SLOTS, ROWS, WIDTH), BF16),
            pltpu.VMEM((RANK, SLOTS * ROWS), BF16),
            pltpu.VMEM((BINS, RANK, SLOTS * ROWS), BF16),
            pltpu.VMEM((BINS, SLOTS * RANK, SHARD), BF16),
            pltpu.SemaphoreType.DMA((7,)),
            pltpu.SemaphoreType.DMA((2,)),
            pltpu.SemaphoreType.DMA((2,)),
            pltpu.SemaphoreType.DMA((2,)),
            pltpu.SemaphoreType.DMA((2,)),
            pltpu.SemaphoreType.DMA((2,)),
        ],
        compiler_params=pltpu.CompilerParams(
            collective_id=0, has_side_effects=True, vmem_limit_bytes=40 << 20
        ),
        name="owner",
    )(hold(index), hold(documents), counts, hold(up), hold(down), hold(cotangent), hold(qkv))


def sum_kernel(
    index_ref, delta_in, grad_ref, per_up_ref,
    delta_out, down_out, up_out,
    down_sum, up_sum, sem,
):
    delta_copy = pltpu.make_async_copy(delta_in, delta_out, sem.at[0])
    delta_copy.start()
    down_copy = pltpu.make_async_copy(down_sum, down_out, sem.at[1])
    up_copy = pltpu.make_async_copy(up_sum, up_out, sem.at[2])
    up_sum[...] = jnp.zeros_like(up_sum)

    def add_up(owner, _):
        for slot in range(SLOTS):
            up_sum[index_ref[slot, owner]] += per_up_ref[owner * SLOTS + slot]
        return 0

    lax.fori_loop(0, BINS, add_up, 0)
    up_copy.start()
    down_sum[...] = jnp.zeros_like(down_sum)

    def add_down(owner, _):
        for slot in range(SLOTS):
            part = grad_ref[owner, slot * RANK : (slot + 1) * RANK]
            down_sum[index_ref[slot, owner]] += part.astype(F32)
        return 0

    lax.fori_loop(0, BINS, add_down, 0)
    down_copy.start()
    delta_copy.wait()
    up_copy.wait()
    down_copy.wait()


def sum_call(index, delta, grad, per_up):
    vmem, hbm = pl.BlockSpec(memory_space=pltpu.VMEM), pl.BlockSpec(memory_space=pl.ANY)
    adapters = jax.ShapeDtypeStruct((ADAPTERS, RANK, SHARD), F32)
    return pl.pallas_call(
        sum_kernel,
        out_shape=(jax.ShapeDtypeStruct(delta.shape, BF16), adapters, adapters),
        in_specs=[pl.BlockSpec(memory_space=pltpu.SMEM), hbm, vmem, vmem],
        out_specs=(hbm, hbm, hbm),
        scratch_shapes=[
            pltpu.VMEM(adapters.shape, F32),
            pltpu.VMEM(adapters.shape, F32),
            pltpu.SemaphoreType.DMA((3,)),
        ],
        compiler_params=pltpu.CompilerParams(vmem_limit_bytes=16 << 20),
        name="sum",
    )(index, delta, grad, per_up)


def on_device(
    query_key_value_blocks,
    row_document_index,
    counts,
    block_adapter_index,
    lowrank_down_weight,
    lowrank_up_weight,
    cotangent,
):
    index = block_adapter_index[0].T
    up = lowrank_up_weight[0]
    down = lowrank_down_weight[0].transpose(0, 2, 1)
    cot = cotangent.reshape(BLOCKS, ROWS, SHARD)
    grad, delta, per_up = owner_call(
        index, row_document_index[0, 0], counts, up, down, cot, query_key_value_blocks[0, 0]
    )
    delta, grad_down, grad_up = sum_call(index, delta, grad, per_up)
    return (
        delta.reshape(cotangent.shape),
        grad_down.transpose(0, 2, 1)[None],
        grad_up[None],
    )


def solution(mesh):
    in_specs = (
        P("phase", "dp", None, None, None),
        P("phase", "dp", None, None),
        P("phase", "dp"),
        P("phase", None, None),
        P("phase", None, "dp", None),
        P("phase", None, None, "dp"),
        P("phase", None, None, None, "dp"),
    )
    out_specs = (
        P("phase", None, None, None, "dp"),
        P("phase", None, "dp", None),
        P("phase", None, None, "dp"),
    )
    return jax.shard_map(
        on_device, mesh=mesh, in_specs=in_specs, out_specs=out_specs, check_vma=False
    )
```

```python
import math

import jax
import jax.numpy as jnp
from jax import lax
from jax.experimental import pallas as pl
from jax.experimental.pallas import tpu as pltpu
from jax.sharding import PartitionSpec as P

HEADS = 64
KV_HEADS = 8
HEAD_DIM = 128
GROUP = HEADS // KV_HEADS
WIDTH = HEADS * HEAD_DIM
RANK = 64
ROWS = 128
SLOTS = 2
SECTIONS = 4
BINS = 32
BLOCKS = BINS * SLOTS
SHARD = WIDTH // BINS
ADAPTERS = 32
LOWRANK_SCALE = 2.0
MESH = pl.DeviceIdType.MESH
F32 = jnp.float32
BF16 = jnp.bfloat16


def hold(array):
    return pltpu.with_memory_space_constraint(array, pltpu.HBM)


def dot(a, b, ca, cb):
    return lax.dot_general(
        a, b, (((ca,), (cb,)), ((), ())), preferred_element_type=F32
    )


def displaced(me, step, sign):
    step = BINS - 1 - step
    kx, turn = step % 4, (step // 4) % 4
    ky, kz = (turn + 4 - kx) % 4, (step // 16 + turn + kx) % 2
    x, y, z = me // 8, (me // 2) % 4, me % 2
    return ((x + 4 + sign * kx) % 4) * 8 + ((y + 4 + sign * ky) % 4) * 2 + (z + kz) % 2


def partner(me, step):
    return displaced(me, step, 1)


def origin(me, step):
    return displaced(me, step, -1)


def owner_kernel(
    index_hbm, documents_hbm, counts_hbm, up_hbm, down_hbm, cot_hbm, qkv_hbm,
    grad_out, delta_out, per_up_out,
    index_ref, counts_ref, up_ref, down_ref, cot, qkv, documents_own, info_own, info_in, bias,
    back_send, back_recv, down_send, down_recv, mixed, scaled, scaled_in, grad_send,
    load_sem, info_sem, back_sem, down_sem, down_sent, scaled_sem, grad_sem,
):
    phase, me = lax.axis_index("phase"), lax.axis_index("dp")
    owners, shards = (phase + SECTIONS - 1) % SECTIONS, (phase + 1) % SECTIONS

    def remote(src, dst, sem, section, to):
        return pltpu.make_async_remote_copy(
            src_ref=src, dst_ref=dst, send_sem=sem.at[0], recv_sem=sem.at[1],
            device_id=(section, to), device_id_type=MESH,
        )

    loads = [
        pltpu.make_async_copy(src, dst, load_sem.at[i])
        for i, (src, dst) in enumerate(
            (
                (index_hbm, index_ref),
                (counts_hbm, counts_ref),
                (documents_hbm, documents_own),
                (down_hbm, down_ref),
                (up_hbm, up_ref),
                (cot_hbm, cot),
                (qkv_hbm, qkv),
            )
        )
    ]
    for load in loads:
        load.start()
    index_load, counts_load, documents_load, down_load, up_load, cot_load, qkv_load = loads

    barrier = pltpu.get_barrier_semaphore()

    def greet(step, _):
        pl.semaphore_signal(
            barrier, inc=1, device_id=(shards, partner(me, step)), device_id_type=MESH
        )
        return 0

    lax.fori_loop(0, BINS, greet, 0)

    counts_load.wait()
    documents_load.wait()
    info_own[...] = jnp.full(info_own.shape, counts_ref[0, 0], jnp.int32)
    info_own[:SLOTS] = documents_own[...]
    index_load.wait()
    down_load.wait()

    def choose_down(to, _):
        for slot in range(SLOTS):
            down_send[to, slot * RANK : (slot + 1) * RANK] = down_ref[index_ref[slot, to]]
        return 0

    lax.fori_loop(0, BINS, choose_down, 0, unroll=4)

    pl.semaphore_wait(barrier, BINS)
    info_copy = remote(info_own, info_in, info_sem, owners, me)
    info_copy.start()

    def down_copy(to, source):
        return pltpu.make_async_remote_copy(
            src_ref=down_send.at[to], dst_ref=down_recv.at[source], send_sem=down_sent, recv_sem=down_sem.at[source],
            device_id=(owners, to), device_id_type=MESH,
        )

    def send_down(step, _):
        to = partner(me, step)
        down_copy(to, me).start()
        return 0


    up_load.wait()
    cot_load.wait()

    def send_back(step, _):
        to = partner(me, step)
        for slot in range(SLOTS):
            part = dot(up_ref[index_ref[slot, to]], cot[to * SLOTS + slot], 1, 1)
            back_send[to, :, slot * ROWS : (slot + 1) * ROWS] = part.astype(BF16)
        remote(back_send.at[to], back_recv.at[me], back_sem, owners, to).start()
        return 0

    lax.fori_loop(0, BINS, send_back, 0, unroll=4)

    lax.fori_loop(0, BINS, send_down, 0)

    info_copy.wait()
    row = lax.broadcasted_iota(jnp.int32, (ROWS, ROWS), 0)
    column = lax.broadcasted_iota(jnp.int32, (ROWS, ROWS), 1)
    for slot in range(SLOTS):
        documents = jnp.broadcast_to(info_in[slot : slot + 1, :].astype(F32), (ROWS, ROWS))
        kept = (documents == documents.T) & (column <= row)
        bias[slot] = jnp.where(kept, 0.0, -1e30)
    qkv_load.wait()
    to_power_of_two = math.log2(math.e) * HEAD_DIM**-0.5

    def attend(step, _):
        slot, kv = step // KV_HEADS, step % KV_HEADS
        alive = jnp.where(info_in[SLOTS : SLOTS + 1, :] > slot, 1.0, 0.0)
        keys = qkv[slot, :, pl.ds(pl.multiple_of(WIDTH + kv * HEAD_DIM, HEAD_DIM), HEAD_DIM)]
        values = qkv[
            slot, :, pl.ds(pl.multiple_of(WIDTH + (KV_HEADS + kv) * HEAD_DIM, HEAD_DIM), HEAD_DIM)
        ]
        heads = [
            pl.ds(pl.multiple_of((kv * GROUP + head) * HEAD_DIM, HEAD_DIM), HEAD_DIM)
            for head in range(GROUP)
        ]
        queries = jnp.concatenate([qkv[slot, :, at] for at in heads], axis=0)
        scores = dot(queries, keys, 1, 1).reshape(GROUP, ROWS, ROWS) + bias[slot]
        top = jnp.max(scores, axis=-1, keepdims=True)
        powers = jnp.exp2((scores - top) * to_power_of_two)
        weights = powers * (1.0 / jnp.sum(powers, axis=-1, keepdims=True))
        weights = weights.astype(BF16).reshape(GROUP * ROWS, ROWS)
        group = (dot(weights, values, 1, 0) * alive).astype(BF16)
        for head, at in enumerate(heads):
            mixed[slot, :, at] = group[head * ROWS : (head + 1) * ROWS]
        return 0

    lax.fori_loop(0, SLOTS * KV_HEADS, attend, 0, unroll=2)

    def piece(which):
        at = pl.ds(pl.multiple_of(which * SHARD, SHARD), SHARD)
        return mixed[:, :, at].reshape(SLOTS * ROWS, SHARD)

    remote(back_send, back_recv, back_sem, owners, me).wait_recv()

    def add_back(source, total):
        return total + back_recv[source].astype(F32)

    back = lax.fori_loop(0, BINS, add_back, jnp.zeros((RANK, SLOTS * ROWS), F32), unroll=4)
    back_scaled = (LOWRANK_SCALE * back).astype(BF16)
    nothing = jnp.zeros((RANK, ROWS), BF16)
    back_diagonal = jnp.concatenate(
        [
            jnp.concatenate([back_scaled[:, :ROWS], nothing], axis=1),
            jnp.concatenate([nothing, back_scaled[:, ROWS:]], axis=1),
        ],
        axis=0,
    )

    def make_grad(to, _):
        grad_send[to] = dot(back_diagonal, piece(to), 1, 0).astype(BF16)
        return 0

    lax.fori_loop(0, BINS, make_grad, 0, unroll=4)

    def project(step, total):
        source = origin(me, step)
        down_copy(source, source).wait_recv()
        return total + dot(down_recv[source], piece(source), 1, 1)

    projected = lax.fori_loop(
        0, BINS, project, jnp.zeros((SLOTS * RANK, SLOTS * ROWS), F32), unroll=4
    )
    for slot in range(SLOTS):
        at = slice(slot * ROWS, (slot + 1) * ROWS)
        own = projected[slot * RANK : (slot + 1) * RANK, at]
        scaled[:, at] = (LOWRANK_SCALE * own).astype(BF16)

    def send_scaled(step, _):
        to = partner(me, step)
        remote(scaled, scaled_in.at[me], scaled_sem, shards, to).start()
        return 0

    lax.fori_loop(0, BINS, send_scaled, 0)

    def send_grad(step, _):
        to = partner(me, step)
        remote(grad_send.at[to], grad_out.at[me], grad_sem, shards, to).start()
        return 0

    lax.fori_loop(0, BINS, send_grad, 0)

    whole_scaled = remote(back_send, scaled_in, scaled_sem, shards, me)
    whole_scaled.wait_recv()

    def spread(source, _):
        for slot in range(SLOTS):
            block = source * SLOTS + slot
            own = scaled_in[source, :, slot * ROWS : (slot + 1) * ROWS]
            delta_out[block] = dot(own, up_ref[index_ref[slot, source]], 0, 0).astype(BF16)
            per_up_out[block] = dot(own, cot[block], 1, 0)
        return 0

    lax.fori_loop(0, BINS, spread, 0, unroll=2)

    remote(back_send, back_recv, back_sem, owners, me).wait_send()
    pltpu.make_async_remote_copy(
        src_ref=down_send, dst_ref=down_recv, send_sem=down_sent, recv_sem=down_sem.at[0],
        device_id=(owners, me), device_id_type=MESH,
    ).wait_send()
    whole_scaled.wait_send()
    whole_grad = remote(grad_send, grad_out, grad_sem, shards, me)
    whole_grad.wait_recv()
    whole_grad.wait_send()


def owner_call(index, documents, counts, up, down, cotangent, qkv):
    vmem, hbm = pl.BlockSpec(memory_space=pltpu.VMEM), pl.BlockSpec(memory_space=pl.ANY)
    return pl.pallas_call(
        owner_kernel,
        out_shape=(
            jax.ShapeDtypeStruct((BINS, SLOTS * RANK, SHARD), BF16),
            jax.ShapeDtypeStruct((BLOCKS, ROWS, SHARD), BF16),
            jax.ShapeDtypeStruct((BLOCKS, RANK, SHARD), F32),
        ),
        in_specs=[pl.BlockSpec(memory_space=pltpu.HBM)] * 7,
        out_specs=(hbm, vmem, vmem),
        scratch_shapes=[
            pltpu.SMEM((SLOTS, BINS), jnp.int32),
            pltpu.SMEM((1, 1), jnp.int32),
            pltpu.VMEM((ADAPTERS, RANK, SHARD), BF16),
            pltpu.VMEM((ADAPTERS, RANK, SHARD), BF16),
            pltpu.VMEM((BLOCKS, ROWS, SHARD), BF16),
            pltpu.VMEM(qkv.shape, BF16),
            pltpu.VMEM((SLOTS, ROWS), jnp.int32),
            pltpu.VMEM((8, ROWS), jnp.int32),
            pltpu.VMEM((8, ROWS), jnp.int32),
            pltpu.VMEM((SLOTS, ROWS, ROWS), F32),
            pltpu.VMEM((BINS, RANK, SLOTS * ROWS), BF16),
            pltpu.VMEM((BINS, RANK, SLOTS * ROWS), BF16),
            pltpu.VMEM((BINS, SLOTS * RANK, SHARD), BF16),
            pltpu.VMEM((BINS, SLOTS * RANK, SHARD), BF16),
            pltpu.VMEM((SLOTS, ROWS, WIDTH), BF16),
            pltpu.VMEM((RANK, SLOTS * ROWS), BF16),
            pltpu.VMEM((BINS, RANK, SLOTS * ROWS), BF16),
            pltpu.VMEM((BINS, SLOTS * RANK, SHARD), BF16),
            pltpu.SemaphoreType.DMA((7,)),
            pltpu.SemaphoreType.DMA((2,)),
            pltpu.SemaphoreType.DMA((2,)),
            pltpu.SemaphoreType.DMA((BINS,)),
            pltpu.SemaphoreType.DMA,
            pltpu.SemaphoreType.DMA((2,)),
            pltpu.SemaphoreType.DMA((2,)),
        ],
        compiler_params=pltpu.CompilerParams(
            collective_id=0, has_side_effects=True, vmem_limit_bytes=40 << 20
        ),
        name="owner",
    )(hold(index), hold(documents), counts, hold(up), hold(down), hold(cotangent), hold(qkv))


def sum_kernel(
    index_ref, delta_in, grad_ref, per_up_ref,
    delta_out, down_out, up_out,
    down_sum, up_sum, sem,
):
    delta_copy = pltpu.make_async_copy(delta_in, delta_out, sem.at[0])
    delta_copy.start()
    down_copy = pltpu.make_async_copy(down_sum, down_out, sem.at[1])
    up_copy = pltpu.make_async_copy(up_sum, up_out, sem.at[2])
    up_sum[...] = jnp.zeros_like(up_sum)
    down_sum[...] = jnp.zeros_like(down_sum)

    def add(owner, _):
        for slot in range(SLOTS):
            adapter = index_ref[slot, owner]
            up_sum[adapter] += per_up_ref[owner * SLOTS + slot]
            part = grad_ref[owner, slot * RANK : (slot + 1) * RANK]
            down_sum[adapter] += part.astype(F32)
        return 0

    lax.fori_loop(0, BINS, add, 0)
    up_copy.start()
    down_copy.start()
    delta_copy.wait()
    up_copy.wait()
    down_copy.wait()


def sum_call(index, delta, grad, per_up):
    vmem, hbm = pl.BlockSpec(memory_space=pltpu.VMEM), pl.BlockSpec(memory_space=pl.ANY)
    adapters = jax.ShapeDtypeStruct((ADAPTERS, RANK, SHARD), F32)
    return pl.pallas_call(
        sum_kernel,
        out_shape=(jax.ShapeDtypeStruct(delta.shape, BF16), adapters, adapters),
        in_specs=[pl.BlockSpec(memory_space=pltpu.SMEM), hbm, vmem, vmem],
        out_specs=(hbm, hbm, hbm),
        scratch_shapes=[
            pltpu.VMEM(adapters.shape, F32),
            pltpu.VMEM(adapters.shape, F32),
            pltpu.SemaphoreType.DMA((3,)),
        ],
        compiler_params=pltpu.CompilerParams(vmem_limit_bytes=16 << 20),
        name="sum",
    )(index, delta, grad, per_up)


def on_device(
    query_key_value_blocks,
    row_document_index,
    counts,
    block_adapter_index,
    lowrank_down_weight,
    lowrank_up_weight,
    cotangent,
):
    index = block_adapter_index[0].T
    up = lowrank_up_weight[0]
    down = lowrank_down_weight[0].transpose(0, 2, 1)
    cot = cotangent.reshape(BLOCKS, ROWS, SHARD)
    grad, delta, per_up = owner_call(
        index, row_document_index[0, 0], counts, up, down, cot, query_key_value_blocks[0, 0]
    )
    delta, grad_down, grad_up = sum_call(index, delta, grad, per_up)
    return (
        delta.reshape(cotangent.shape),
        grad_down.transpose(0, 2, 1)[None],
        grad_up[None],
    )


def solution(mesh):
    in_specs = (
        P("phase", "dp", None, None, None),
        P("phase", "dp", None, None),
        P("phase", "dp"),
        P("phase", None, None),
        P("phase", None, "dp", None),
        P("phase", None, None, "dp"),
        P("phase", None, None, None, "dp"),
    )
    out_specs = (
        P("phase", None, None, None, "dp"),
        P("phase", None, "dp", None),
        P("phase", None, None, "dp"),
    )
    return jax.shard_map(
        on_device, mesh=mesh, in_specs=in_specs, out_specs=out_specs, check_vma=False
    )
```

```python
import math

import jax
import jax.numpy as jnp
from jax import lax
from jax.experimental import pallas as pl
from jax.experimental.pallas import tpu as pltpu
from jax.sharding import PartitionSpec as P

HEADS = 64
KV_HEADS = 8
HEAD_DIM = 128
GROUP = HEADS // KV_HEADS
WIDTH = HEADS * HEAD_DIM
RANK = 64
ROWS = 128
SLOTS = 2
SECTIONS = 4
BINS = 32
BLOCKS = BINS * SLOTS
SHARD = WIDTH // BINS
ADAPTERS = 32
LOWRANK_SCALE = 2.0
MESH = pl.DeviceIdType.MESH
F32 = jnp.float32
BF16 = jnp.bfloat16


def hold(array):
    return pltpu.with_memory_space_constraint(array, pltpu.HBM)


def dot(a, b, ca, cb):
    return lax.dot_general(
        a, b, (((ca,), (cb,)), ((), ())), preferred_element_type=F32
    )


def displaced(me, step, sign):
    step = BINS - 1 - step
    kx, turn = step % 4, (step // 4) % 4
    ky, kz = (turn + 4 - kx) % 4, (step // 16 + turn + kx) % 2
    x, y, z = me // 8, (me // 2) % 4, me % 2
    return ((x + 4 + sign * kx) % 4) * 8 + ((y + 4 + sign * ky) % 4) * 2 + (z + kz) % 2


def partner(me, step):
    return displaced(me, step, 1)


def origin(me, step):
    return displaced(me, step, -1)


def owner_kernel(
    index_hbm, documents_hbm, counts_hbm, up_hbm, down_hbm, cot_hbm, qkv_hbm,
    grad_out, delta_out, per_up_out,
    index_ref, counts_ref, up_ref, down_ref, cot, qkv, documents_own, info_own, info_in, bias,
    back_send, back_recv, down_send, down_recv, mixed, scaled, scaled_in, grad_send,
    load_sem, info_sem, back_sem, down_sem, down_sent, scaled_sem, grad_sem,
):
    phase, me = lax.axis_index("phase"), lax.axis_index("dp")
    owners, shards = (phase + SECTIONS - 1) % SECTIONS, (phase + 1) % SECTIONS

    def remote(src, dst, sem, section, to):
        return pltpu.make_async_remote_copy(
            src_ref=src, dst_ref=dst, send_sem=sem.at[0], recv_sem=sem.at[1],
            device_id=(section, to), device_id_type=MESH,
        )

    loads = [
        pltpu.make_async_copy(src, dst, load_sem.at[i])
        for i, (src, dst) in enumerate(
            (
                (index_hbm, index_ref),
                (counts_hbm, counts_ref),
                (documents_hbm, documents_own),
                (down_hbm, down_ref),
                (up_hbm, up_ref),
                (cot_hbm, cot),
                (qkv_hbm, qkv),
            )
        )
    ]
    for load in loads:
        load.start()
    index_load, counts_load, documents_load, down_load, up_load, cot_load, qkv_load = loads

    barrier = pltpu.get_barrier_semaphore()

    def greet(step, _):
        pl.semaphore_signal(
            barrier, inc=1, device_id=(shards, partner(me, step)), device_id_type=MESH
        )
        return 0

    lax.fori_loop(0, BINS, greet, 0)

    counts_load.wait()
    documents_load.wait()
    info_own[...] = jnp.full(info_own.shape, counts_ref[0, 0], jnp.int32)
    info_own[:SLOTS] = documents_own[...]
    index_load.wait()

    pl.semaphore_wait(barrier, BINS)
    info_copy = remote(info_own, info_in, info_sem, owners, me)
    info_copy.start()

    def down_copy(to, source):
        return pltpu.make_async_remote_copy(
            src_ref=down_send.at[to], dst_ref=down_recv.at[source], send_sem=down_sent, recv_sem=down_sem.at[source],
            device_id=(owners, to), device_id_type=MESH,
        )

    def send_down(step, _):
        to = partner(me, step)
        down_copy(to, me).start()
        return 0


    up_load.wait()
    cot_load.wait()

    def send_back(step, _):
        to = partner(me, step)
        for slot in range(SLOTS):
            part = dot(up_ref[index_ref[slot, to]], cot[to * SLOTS + slot], 1, 1)
            back_send[to, :, slot * ROWS : (slot + 1) * ROWS] = part.astype(BF16)
        remote(back_send.at[to], back_recv.at[me], back_sem, owners, to).start()
        return 0

    lax.fori_loop(0, BINS, send_back, 0, unroll=4)

    down_load.wait()

    def choose_down(to, _):
        for slot in range(SLOTS):
            down_send[to, slot * RANK : (slot + 1) * RANK] = down_ref[index_ref[slot, to]]
        return 0

    lax.fori_loop(0, BINS, choose_down, 0, unroll=4)

    lax.fori_loop(0, BINS, send_down, 0)

    info_copy.wait()
    row = lax.broadcasted_iota(jnp.int32, (ROWS, ROWS), 0)
    column = lax.broadcasted_iota(jnp.int32, (ROWS, ROWS), 1)
    for slot in range(SLOTS):
        documents = jnp.broadcast_to(info_in[slot : slot + 1, :].astype(F32), (ROWS, ROWS))
        kept = (documents == documents.T) & (column <= row)
        bias[slot] = jnp.where(kept, 0.0, -1e30)
    qkv_load.wait()
    to_power_of_two = math.log2(math.e) * HEAD_DIM**-0.5

    def attend(step, _):
        slot, kv = step // KV_HEADS, step % KV_HEADS
        alive = jnp.where(info_in[SLOTS : SLOTS + 1, :] > slot, 1.0, 0.0)
        keys = qkv[slot, :, pl.ds(pl.multiple_of(WIDTH + kv * HEAD_DIM, HEAD_DIM), HEAD_DIM)]
        values = qkv[
            slot, :, pl.ds(pl.multiple_of(WIDTH + (KV_HEADS + kv) * HEAD_DIM, HEAD_DIM), HEAD_DIM)
        ]
        heads = [
            pl.ds(pl.multiple_of((kv * GROUP + head) * HEAD_DIM, HEAD_DIM), HEAD_DIM)
            for head in range(GROUP)
        ]
        queries = jnp.concatenate([qkv[slot, :, at] for at in heads], axis=0)
        scores = dot(queries, keys, 1, 1).reshape(GROUP, ROWS, ROWS) + bias[slot]
        top = jnp.max(scores, axis=-1, keepdims=True)
        powers = jnp.exp2((scores - top) * to_power_of_two)
        weights = powers * (1.0 / jnp.sum(powers, axis=-1, keepdims=True))
        weights = weights.astype(BF16).reshape(GROUP * ROWS, ROWS)
        group = (dot(weights, values, 1, 0) * alive).astype(BF16)
        for head, at in enumerate(heads):
            mixed[slot, :, at] = group[head * ROWS : (head + 1) * ROWS]
        return 0

    lax.fori_loop(0, SLOTS * KV_HEADS, attend, 0, unroll=2)

    def piece(which):
        at = pl.ds(pl.multiple_of(which * SHARD, SHARD), SHARD)
        return mixed[:, :, at].reshape(SLOTS * ROWS, SHARD)

    remote(back_send, back_recv, back_sem, owners, me).wait_recv()

    def add_back(source, total):
        return total + back_recv[source].astype(F32)

    back = lax.fori_loop(0, BINS, add_back, jnp.zeros((RANK, SLOTS * ROWS), F32), unroll=4)
    back_scaled = (LOWRANK_SCALE * back).astype(BF16)
    nothing = jnp.zeros((RANK, ROWS), BF16)
    back_diagonal = jnp.concatenate(
        [
            jnp.concatenate([back_scaled[:, :ROWS], nothing], axis=1),
            jnp.concatenate([nothing, back_scaled[:, ROWS:]], axis=1),
        ],
        axis=0,
    )

    def make_grad(to, _):
        grad_send[to] = dot(back_diagonal, piece(to), 1, 0).astype(BF16)
        return 0

    lax.fori_loop(0, BINS, make_grad, 0, unroll=4)

    def project(step, total):
        source = origin(me, step)
        down_copy(source, source).wait_recv()
        return total + dot(down_recv[source], piece(source), 1, 1)

    projected = lax.fori_loop(
        0, BINS, project, jnp.zeros((SLOTS * RANK, SLOTS * ROWS), F32), unroll=4
    )
    for slot in range(SLOTS):
        at = slice(slot * ROWS, (slot + 1) * ROWS)
        own = projected[slot * RANK : (slot + 1) * RANK, at]
        scaled[:, at] = (LOWRANK_SCALE * own).astype(BF16)

    def send_scaled(step, _):
        to = partner(me, step)
        remote(scaled, scaled_in.at[me], scaled_sem, shards, to).start()
        return 0

    lax.fori_loop(0, BINS, send_scaled, 0)

    def send_grad(step, _):
        to = partner(me, step)
        remote(grad_send.at[to], grad_out.at[me], grad_sem, shards, to).start()
        return 0

    lax.fori_loop(0, BINS, send_grad, 0)

    whole_scaled = remote(back_send, scaled_in, scaled_sem, shards, me)
    whole_scaled.wait_recv()

    def spread(source, _):
        for slot in range(SLOTS):
            block = source * SLOTS + slot
            own = scaled_in[source, :, slot * ROWS : (slot + 1) * ROWS]
            delta_out[block] = dot(own, up_ref[index_ref[slot, source]], 0, 0).astype(BF16)
            per_up_out[block] = dot(own, cot[block], 1, 0)
        return 0

    lax.fori_loop(0, BINS, spread, 0, unroll=2)

    remote(back_send, back_recv, back_sem, owners, me).wait_send()
    pltpu.make_async_remote_copy(
        src_ref=down_send, dst_ref=down_recv, send_sem=down_sent, recv_sem=down_sem.at[0],
        device_id=(owners, me), device_id_type=MESH,
    ).wait_send()
    whole_scaled.wait_send()
    whole_grad = remote(grad_send, grad_out, grad_sem, shards, me)
    whole_grad.wait_recv()
    whole_grad.wait_send()


def owner_call(index, documents, counts, up, down, cotangent, qkv):
    vmem, hbm = pl.BlockSpec(memory_space=pltpu.VMEM), pl.BlockSpec(memory_space=pl.ANY)
    return pl.pallas_call(
        owner_kernel,
        out_shape=(
            jax.ShapeDtypeStruct((BINS, SLOTS * RANK, SHARD), BF16),
            jax.ShapeDtypeStruct((BLOCKS, ROWS, SHARD), BF16),
            jax.ShapeDtypeStruct((BLOCKS, RANK, SHARD), F32),
        ),
        in_specs=[pl.BlockSpec(memory_space=pltpu.HBM)] * 7,
        out_specs=(hbm, vmem, vmem),
        scratch_shapes=[
            pltpu.SMEM((SLOTS, BINS), jnp.int32),
            pltpu.SMEM((1, 1), jnp.int32),
            pltpu.VMEM((ADAPTERS, RANK, SHARD), BF16),
            pltpu.VMEM((ADAPTERS, RANK, SHARD), BF16),
            pltpu.VMEM((BLOCKS, ROWS, SHARD), BF16),
            pltpu.VMEM(qkv.shape, BF16),
            pltpu.VMEM((SLOTS, ROWS), jnp.int32),
            pltpu.VMEM((8, ROWS), jnp.int32),
            pltpu.VMEM((8, ROWS), jnp.int32),
            pltpu.VMEM((SLOTS, ROWS, ROWS), F32),
            pltpu.VMEM((BINS, RANK, SLOTS * ROWS), BF16),
            pltpu.VMEM((BINS, RANK, SLOTS * ROWS), BF16),
            pltpu.VMEM((BINS, SLOTS * RANK, SHARD), BF16),
            pltpu.VMEM((BINS, SLOTS * RANK, SHARD), BF16),
            pltpu.VMEM((SLOTS, ROWS, WIDTH), BF16),
            pltpu.VMEM((RANK, SLOTS * ROWS), BF16),
            pltpu.VMEM((BINS, RANK, SLOTS * ROWS), BF16),
            pltpu.VMEM((BINS, SLOTS * RANK, SHARD), BF16),
            pltpu.SemaphoreType.DMA((7,)),
            pltpu.SemaphoreType.DMA((2,)),
            pltpu.SemaphoreType.DMA((2,)),
            pltpu.SemaphoreType.DMA((BINS,)),
            pltpu.SemaphoreType.DMA,
            pltpu.SemaphoreType.DMA((2,)),
            pltpu.SemaphoreType.DMA((2,)),
        ],
        compiler_params=pltpu.CompilerParams(
            collective_id=0, has_side_effects=True, vmem_limit_bytes=40 << 20
        ),
        name="owner",
    )(hold(index), hold(documents), counts, hold(up), hold(down), hold(cotangent), hold(qkv))


def sum_kernel(
    index_ref, delta_in, grad_ref, per_up_ref,
    delta_out, down_out, up_out,
    down_sum, up_sum, sem,
):
    delta_copy = pltpu.make_async_copy(delta_in, delta_out, sem.at[0])
    delta_copy.start()
    down_copy = pltpu.make_async_copy(down_sum, down_out, sem.at[1])
    up_copy = pltpu.make_async_copy(up_sum, up_out, sem.at[2])
    up_sum[...] = jnp.zeros_like(up_sum)
    down_sum[...] = jnp.zeros_like(down_sum)

    def add(owner, _):
        for slot in range(SLOTS):
            adapter = index_ref[slot, owner]
            up_sum[adapter] += per_up_ref[owner * SLOTS + slot]
            part = grad_ref[owner, slot * RANK : (slot + 1) * RANK]
            down_sum[adapter] += part.astype(F32)
        return 0

    lax.fori_loop(0, BINS, add, 0)
    up_copy.start()
    down_copy.start()
    delta_copy.wait()
    up_copy.wait()
    down_copy.wait()


def sum_call(index, delta, grad, per_up):
    vmem, hbm = pl.BlockSpec(memory_space=pltpu.VMEM), pl.BlockSpec(memory_space=pl.ANY)
    adapters = jax.ShapeDtypeStruct((ADAPTERS, RANK, SHARD), F32)
    return pl.pallas_call(
        sum_kernel,
        out_shape=(jax.ShapeDtypeStruct(delta.shape, BF16), adapters, adapters),
        in_specs=[pl.BlockSpec(memory_space=pltpu.SMEM), hbm, vmem, vmem],
        out_specs=(hbm, hbm, hbm),
        scratch_shapes=[
            pltpu.VMEM(adapters.shape, F32),
            pltpu.VMEM(adapters.shape, F32),
            pltpu.SemaphoreType.DMA((3,)),
        ],
        compiler_params=pltpu.CompilerParams(vmem_limit_bytes=16 << 20),
        name="sum",
    )(index, delta, grad, per_up)


def on_device(
    query_key_value_blocks,
    row_document_index,
    counts,
    block_adapter_index,
    lowrank_down_weight,
    lowrank_up_weight,
    cotangent,
):
    index = block_adapter_index[0].T
    up = lowrank_up_weight[0]
    down = lowrank_down_weight[0].transpose(0, 2, 1)
    cot = cotangent.reshape(BLOCKS, ROWS, SHARD)
    grad, delta, per_up = owner_call(
        index, row_document_index[0, 0], counts, up, down, cot, query_key_value_blocks[0, 0]
    )
    delta, grad_down, grad_up = sum_call(index, delta, grad, per_up)
    return (
        delta.reshape(cotangent.shape),
        grad_down.transpose(0, 2, 1)[None],
        grad_up[None],
    )


def solution(mesh):
    in_specs = (
        P("phase", "dp", None, None, None),
        P("phase", "dp", None, None),
        P("phase", "dp"),
        P("phase", None, None),
        P("phase", None, "dp", None),
        P("phase", None, None, "dp"),
        P("phase", None, None, None, "dp"),
    )
    out_specs = (
        P("phase", None, None, None, "dp"),
        P("phase", None, "dp", None),
        P("phase", None, None, "dp"),
    )
    return jax.shard_map(
        on_device, mesh=mesh, in_specs=in_specs, out_specs=out_specs, check_vma=False
    )
```
